128 devices in a mesh: dp: 2 (over x_lo), mp: 64 (over z, y, x_hi, core).
Axes of the slice: x: 4 (x_hi: 2, x_lo: 2; x = x_hi * 2 + x_lo), y: 4, z: 4, core: 2. Of those that a mesh axis runs over, the one named last changes fastest.
Arguments:
- grad_partials: bfloat16 [2, 64, 1024, 1024], P('dp', None, 'mp'), may hold values from -60 to 60
- second_moment: float32 [64, 1024, 1024], P('mp', None, 'dp'), may hold values from 0.1 to 10
- left_root: float32 [64, 1024, 1024], P('mp', 'dp'), may hold values from -1 to 3
- right_root: float32 [64, 1024, 1024], P('mp', None, 'dp'), may hold values from -1 to 3
- left_stat: float32 [64, 1024, 1024], P('mp', 'dp'), may hold values from -6 to 6
- right_stat: float32 [64, 1024, 1024], P('mp', None, 'dp'), may hold values from -6 to 6
Outputs:
- update: float32 [64, 1024, 1024], P(None, 'mp', 'dp')
- moment_new: float32 [64, 1024, 1024], P('mp', None, 'dp')
- left_new: float32 [64, 1024, 1024], P('mp', 'dp')
- right_new: float32 [64, 1024, 1024], P('mp', None, 'dp')
The draws below stay inside these ranges and needn't reach their ends.
All inputs are finite; a program needn't handle non-finite values.
Results may differ from the reference program's by a relative error of at most 0.0003.
Values may be sent and summed in bfloat16 or wider, within the bound.
No kernel may reach another device: no remote copies, remote signals or barrier semaphores. Data moves between devices by JAX's collectives and lax.ppermute only.
A program may use at most 128 MiB of HBM per device.

```python
import math
import jax
import jax.numpy as jnp
from jax import lax

BS = 1024
BLOCKS = 64
N_DP = 2


def draw_grad_partials(key, part):
    key = jax.random.fold_in(key, 11)
    base_key, col_key, row_key = jax.random.split(key, 3)
    columns = jnp.arange(BS, dtype=jnp.float32) / BS - 0.5
    jitter = jnp.clip(jax.random.normal(col_key, (BLOCKS, 1, BS)), -3.0, 3.0)
    col_scale = jnp.exp(jnp.log(10.0) * columns + 0.35 * jitter)
    row_scale = jnp.exp(jnp.log(10.0) * (jax.random.uniform(row_key, (BLOCKS, BS, 1)) - 0.5))
    values = jnp.clip(jax.random.normal(base_key, (N_DP, BLOCKS, BS, BS)), -6.0, 6.0)
    return (0.35 * values * col_scale * row_scale).astype(jnp.bfloat16)


def draw_left_root(key, part):
    key = jax.random.fold_in(key, 23)
    diag_key, spread_key = jax.random.split(key)
    diagonal = jnp.exp(jnp.log(2.0) * (2.0 * jax.random.uniform(diag_key, (BLOCKS, BS, 1)) - 1.0))
    offdiag = jnp.clip(jax.random.normal(spread_key, (BLOCKS, BS, BS)), -6.0, 6.0) * 0.6
    identity = jnp.eye(BS, dtype=jnp.float32)
    return (identity * diagonal + offdiag / jnp.sqrt(jnp.float32(BS))).astype(jnp.float32)


def draw_right_root(key, part):
    key = jax.random.fold_in(key, 37)
    diag_key, spread_key = jax.random.split(key)
    diagonal = jnp.exp(jnp.log(2.0) * (2.0 * jax.random.uniform(diag_key, (BLOCKS, BS, 1)) - 1.0))
    offdiag = jnp.clip(jax.random.normal(spread_key, (BLOCKS, BS, BS)), -6.0, 6.0) * 0.6
    identity = jnp.eye(BS, dtype=jnp.float32)
    return (identity * diagonal + offdiag / jnp.sqrt(jnp.float32(BS))).astype(jnp.float32)


def levels(stream_key, dims, pieces, smallest, top_value):
    def one(position, blocks):
        draws = jax.random.uniform(jax.random.fold_in(jax.random.fold_in(stream_key, 6), position), (blocks,), jnp.float32, smallest / len(pieces), top_value / len(pieces))
        return jnp.repeat(jnp.exp(draws), dims[position] // blocks).reshape((-1,) + (1,) * (len(dims) - position - 1))

    loudness = one(*pieces[0])
    for cut in pieces[1:]:
        loudness = loudness * one(*cut)
    return loudness


def normal_values(stream_key, extent, spread, limit, cuts=(), kind=jnp.bfloat16):
    loudness = levels(stream_key, extent, cuts, -0.22, 0.18) if cuts else 1.0
    values = jax.random.normal(stream_key, extent, jnp.float32) * spread * loudness
    return jnp.minimum(jnp.maximum(values, -limit), limit).astype(kind)


def setup_inputs(seed: int = 0) -> dict:
    key_of = jax.random.split(jax.random.key(seed), 7)
    return {
        "grad_partials": draw_grad_partials(jax.random.fold_in(key_of[6], 71), 0),
        "second_moment": jnp.clip(jnp.exp(math.log(10.0) - 4.6051702 * jax.random.uniform(key_of[1], (BLOCKS, BS, BS), jnp.float32) ** levels(key_of[1], (BLOCKS, BS, BS), ((0, 64), (2, 2)), -0.2, 0.2)), 0.1, 10.0),
        "left_root": draw_left_root(jax.random.fold_in(key_of[6], 71), 0),
        "right_root": draw_right_root(jax.random.fold_in(key_of[6], 71), 0),
        "left_stat": normal_values(key_of[4], (BLOCKS, BS, BS), 1.0, 6.0, ((0, 64), (1, 2)), jnp.float32),
        "right_stat": normal_values(key_of[5], (BLOCKS, BS, BS), 1.0, 6.0, ((0, 64), (2, 2)), jnp.float32),
    }


MOMENT_DECAY = 0.9
STAT_DECAY = 0.9
ADAM_EPS = 1e-08
NORM_EPS = 1e-06

def highest(form, left, right):
    return jnp.einsum(form, left, right, precision=lax.Precision.HIGHEST, preferred_element_type=jnp.float32)

def one_block(inputs):
    partials, moment, left_root, right_root, left_stat, right_stat = inputs
    gradient = lax.optimization_barrier(jnp.sum(partials.astype(jnp.float32), axis=0))
    moment_new = MOMENT_DECAY * moment + (1.0 - MOMENT_DECAY) * gradient * gradient
    adam_dir = gradient / (jnp.sqrt(moment_new) + ADAM_EPS)
    left_new = STAT_DECAY * left_stat + (1.0 - STAT_DECAY) / BS * highest('ic,jc->ij', gradient, gradient)
    right_new = STAT_DECAY * right_stat + (1.0 - STAT_DECAY) / BS * highest('ri,rj->ij', gradient, gradient)
    product = highest('ij,jc->ic', left_root, gradient)
    shampoo = highest('ic,cj->ij', product, right_root)
    entries = float(BS * BS)
    graft_ratio = jnp.sqrt(jnp.sum(adam_dir * adam_dir) / entries + NORM_EPS) / jnp.sqrt(jnp.sum(shampoo * shampoo) / entries + NORM_EPS)
    return (graft_ratio * shampoo, moment_new, left_new, right_new)

def reference(grad_partials, second_moment, left_root, right_root, left_stat, right_stat):
    blocked = jnp.moveaxis(grad_partials, 1, 0)
    update, moment_new, left_new, right_new = lax.map(one_block, (blocked, second_moment, left_root, right_root, left_stat, right_stat))
    return (update, moment_new, left_new, right_new)
```

```python
import jax
import jax.numpy as jnp
from jax import lax
from jax.experimental import pallas as pl
from jax.experimental.pallas import tpu as pltpu
from jax.sharding import PartitionSpec as P

MOMENT_DECAY = 0.9
STAT_DECAY = 0.9
ADAM_EPS = 1e-08
NORM_EPS = 1e-06
SWAP = [(0, 1), (1, 0)]
TAIL = 16
LANES = 128
POWER = 14
SMALLEST = 1e-30
CHUNKS = 4
EARLY = 9 / 16
F32, BF16 = jnp.float32, jnp.bfloat16


VMEM = pl.BlockSpec(memory_space=pltpu.VMEM)
SMEM = pl.BlockSpec(memory_space=pltpu.SMEM)
ANY = pl.BlockSpec(memory_space=pl.ANY)
HBM = pl.BlockSpec(memory_space=pltpu.HBM)


def params(mebibytes):
    return pltpu.CompilerParams(vmem_limit_bytes=mebibytes * 1024 * 1024)


def near(values):
    return pltpu.with_memory_space_constraint(values, pltpu.VMEM)


def far(values):
    return pltpu.with_memory_space_constraint(values, pltpu.HBM)


def exponent_of(top):
    return jnp.floor(jnp.log2(jnp.maximum(top, SMALLEST))) - 8.0


def encode(scaled):
    square = scaled * scaled
    fourth = square * square
    return (fourth * fourth * fourth * (scaled * jnp.abs(scaled))).astype(BF16)


def decode(coded):
    wide = coded.astype(F32)
    size = jnp.abs(wide)
    root = jnp.exp2(jnp.log2(jnp.maximum(size, 1e-37)) * (1.0 / POWER))
    return jnp.where(size == 0.0, 0.0, jnp.where(wide < 0.0, -root, root))


def split(values):
    high = values.astype(BF16)
    return high, (values - high.astype(F32)).astype(BF16)


def dot3(left, right):
    dot = lambda a, b: jnp.dot(a, b, preferred_element_type=F32)
    return dot(left[0], right[0]) + (dot(left[0], right[1]) + dot(left[1], right[0]))


def fold(values):
    rows, columns = values.shape
    return jnp.sum(values.reshape(rows // 8, 8, columns), axis=0)


def parts_of(rows):
    early = int(rows * EARLY) // 32 * 32
    return ((0, early // 2), (early // 2, early)), ((early, (early + rows) // 2), ((early + rows) // 2, rows))


def pack_kernel(group, left_ref, code_ref, left, sems):
    columns = left.shape[1]
    origin = group[0][0]
    fetches = []
    for start, stop in group:
        here = pl.ds(start - origin, stop - start)
        source = left_ref.at[pl.ds(start, stop - start)]
        fetches.append(pltpu.make_async_copy(source, left.at[here], sems.at[len(fetches)]))
        fetches[-1].start()
    tails = []
    for start, stop in group:
        here = slice(start - origin, stop - origin)
        fetches.pop(0).wait()
        values = left[here]
        exponent = exponent_of(jnp.max(jnp.abs(values), axis=(0, 1), keepdims=True))
        code_ref[here] = encode(values * jnp.exp2(-exponent))
        tails.append(jnp.broadcast_to(exponent, (TAIL, columns // 2)))
    code_ref[left.shape[0] :] = jnp.concatenate(tails, axis=1).astype(BF16)


def pack(left, which):
    columns = left.shape[1]
    group = parts_of(left.shape[0])[which]
    depth = group[1][1] - group[0][0]

    def kernel(*refs):
        pack_kernel(group, *refs)

    return pl.pallas_call(
        kernel,
        in_specs=[HBM],
        out_specs=VMEM,
        out_shape=jax.ShapeDtypeStruct((depth + TAIL, columns), BF16),
        scratch_shapes=[pltpu.VMEM((depth, columns), F32), pltpu.SemaphoreType.DMA((2,))],
        compiler_params=params(16),
    )(far(left))


def root_of(code_ref, group):
    origin, end = group[0][0], group[1][1]
    depth = end - origin
    columns = code_ref.shape[1]
    scales = jnp.exp2(code_ref[depth : depth + TAIL].astype(F32)[0:1])
    rows = []
    for part, (start, stop) in enumerate(group):
        lane = part * (columns // 2)
        rows.append(decode(code_ref[start - origin : stop - origin]) * scales[:, lane : lane + 1])
    return jnp.concatenate(rows, axis=0)


def double_kernel(partials_ref, doubled_ref, partials, turned, fetch_sems, write_sems):
    parts = fetch_sems.shape[0]
    blocks = partials.shape[0]
    per = blocks // parts
    fetches, writes = [], []
    for part in range(parts):
        here = pl.ds(part * per, per)
        fetches.append(pltpu.make_async_copy(partials_ref.at[here], partials.at[here], fetch_sems.at[part]))
        fetches[-1].start()
    for part in range(parts):
        fetches[part].wait()
        for block in range(part * per, (part + 1) * per):
            turned[blocks - 1 - block] = partials[block]
        there = pl.ds(blocks - (part + 1) * per, per)
        for copy in range(2):
            writes.append(
                pltpu.make_async_copy(
                    turned.at[there], doubled_ref.at[there, copy], write_sems.at[2 * part + copy]
                )
            )
            writes[-1].start()
    for write in writes:
        write.wait()


def double(partials):
    blocks, slab, size = partials.shape
    return pl.pallas_call(
        double_kernel,
        in_specs=[HBM],
        out_specs=HBM,
        out_shape=pltpu.HBM((blocks, 2, slab, size), BF16),
        scratch_shapes=[
            pltpu.VMEM(partials.shape, BF16),
            pltpu.VMEM(partials.shape, BF16),
            pltpu.SemaphoreType.DMA((4,)),
            pltpu.SemaphoreType.DMA((8,)),
        ],
        compiler_params=params(16),
    )(far(partials))


def coded(shampoo, slab, sent, facts, first):
    rows, half = shampoo.shape
    messages = rows // slab
    grouped = shampoo.reshape(messages, slab, half)
    exponent = exponent_of(jnp.max(jnp.abs(grouped), axis=(1, 2), keepdims=True))
    code = encode(grouped * jnp.exp2(-exponent))
    wide = jnp.broadcast_to(exponent, (messages, TAIL, LANES)).astype(BF16)
    for message in range(messages):
        place = first + (messages - 1 - message)
        for tile in range(half // LANES):
            sent[place, tile * slab : (tile + 1) * slab, :] = code[
                message, :, tile * LANES : (tile + 1) * LANES
            ]
        facts[place] = wide[message]
    return fold(shampoo * shampoo)


def main_kernel(
    side_ref, right_ref, pieces_ref, moment_ref, left_ref, code_ref,
    grad_ref, new_ref, sent, turn_hi, turn_lo, facts_ref, sums_ref,
    pieces, moment, left, grad, new, right_hi, right_lo, fetch_sems, write_sems,
):
    side = side_ref[0]
    blocks, _, slab, size = pieces.shape
    half = size // 2
    chunks = CHUNKS
    rows = size // chunks
    messages = rows // slab
    early = parts_of(half)[0]

    def fetch(source, target, slot):
        copy = pltpu.make_async_copy(source, target, fetch_sems.at[slot])
        copy.start()
        return copy

    def fetch_pieces(chunk):
        here = pl.ds(blocks - (chunk + 1) * messages, messages)
        return fetch(pieces_ref.at[here], pieces.at[here], chunk)

    def fetch_moment(chunk):
        here = pl.ds(chunk * rows, rows)
        return fetch(moment_ref.at[here], moment.at[here], chunks + chunk)

    piece_arrivals = [fetch_pieces(chunk) for chunk in range(chunks)]
    moment_arrivals = [fetch_moment(chunk) for chunk in range(chunks)]
    writes = []

    def write(source, target):
        writes.append(pltpu.make_async_copy(source, target, write_sems.at[len(writes)]))
        writes[-1].start()

    right_hi[...], right_lo[...] = split(right_ref[...])
    adam = jnp.zeros((8, half), F32)
    for chunk in range(chunks):
        here = slice(chunk * rows, (chunk + 1) * rows)
        piece_arrivals[chunk].wait()
        if chunk == 0:
            left_arrival = fetch(left_ref, left, 2 * chunks)
        for message in range(messages):
            source = chunk * messages + message
            piece = blocks - 1 - source
            grad[source * slab : (source + 1) * slab] = pieces[piece, 0].astype(F32) + pieces[
                piece, 1
            ].astype(F32)
        write(grad.at[pl.ds(chunk * rows, rows)], grad_ref.at[pl.ds(chunk * rows, rows)])
        turned = dot3(split(grad[here]), (right_hi[...], right_lo[...]))
        turn_hi[here], turn_lo[here] = split(turned)
        mine = grad[here, pl.ds(pl.multiple_of(side * half, half), half)]
        moment_arrivals[chunk].wait()
        moment_new = MOMENT_DECAY * moment[here] + (1.0 - MOMENT_DECAY) * mine * mine
        new[here] = moment_new
        direction = mine / (jnp.sqrt(moment_new) + ADAM_EPS)
        adam += fold(direction * direction)
    write(new, new_ref)

    def finish(left, row_block):
        shampoo = dot3(split(left), (turn_hi[...], turn_lo[...]))
        count = left.shape[0] // slab
        first = blocks - count - row_block
        return coded(shampoo, slab, sent, facts_ref, first)

    squares = jnp.zeros((8, half), F32)
    left_arrival.wait()
    for start in range(0, half, rows):
        squares += finish(left[start : start + rows], side * (blocks // 2) + start // slab)
    squares += finish(root_of(code_ref, early), (1 - side) * (blocks // 2))
    sums_ref[:8] = adam
    sums_ref[8:] = squares
    for copy in writes:
        copy.wait()


def main(side, pieces, moment, right, left, code):
    size, half = right.shape
    blocks, _, slab, _ = pieces.shape
    data = half // LANES * slab
    return pl.pallas_call(
        main_kernel,
        in_specs=[SMEM, VMEM, HBM, HBM, HBM, VMEM],
        out_specs=[HBM, ANY, VMEM, VMEM, VMEM, VMEM, VMEM],
        out_shape=[
            pltpu.HBM((size, size), F32),
            jax.ShapeDtypeStruct((size, half), F32),
            pltpu.VMEM((blocks, data, LANES), BF16),
            pltpu.VMEM((size, half), BF16),
            pltpu.VMEM((size, half), BF16),
            pltpu.VMEM((blocks, TAIL, LANES), BF16),
            pltpu.VMEM((16, half), F32),
        ],
        scratch_shapes=[
            pltpu.VMEM(pieces.shape, BF16),
            pltpu.VMEM(moment.shape, F32),
            pltpu.VMEM(left.shape, F32),
            pltpu.VMEM((size, size), F32),
            pltpu.VMEM(moment.shape, F32),
            pltpu.VMEM((size, half), BF16),
            pltpu.VMEM((size, half), BF16),
            pltpu.SemaphoreType.DMA((2 * CHUNKS + 1,)),
            pltpu.SemaphoreType.DMA((CHUNKS + 1,)),
        ],
        compiler_params=params(36),
        cost_estimate=pl.CostEstimate(
            flops=12 * size * size * half, bytes_accessed=16 * size * size, transcendentals=4 * size * half
        ),
    )(side, near(right), far(pieces), far(moment), far(left), near(code))


def last_kernel(side_ref, turn_hi, turn_lo, code_ref, facts_ref, sums_ref, done_ref, sent_ref, sent, facts, sems):
    side = side_ref[0]
    blocks = facts.shape[0]
    slab = 16
    data = sent.shape[1]
    half = turn_hi.shape[1]
    late = parts_of(half)[1]
    count = sent.shape[0]
    row_block = (1 - side) * (blocks // 2) + late[0][0] // slab
    first = blocks - count - row_block

    writes = []

    def write(source, target):
        writes.append(pltpu.make_async_copy(source, target, sems.at[len(writes)]))
        writes[-1].start()

    rest = blocks // 2 - count
    for start, extent in (((1 - side) * (blocks // 2), blocks // 2), (first + count, rest)):
        here = pl.ds(start, extent)
        write(done_ref.at[here], sent_ref.at[here, pl.ds(0, data)])
    facts[...] = facts_ref[...]
    shampoo = dot3(split(root_of(code_ref, late)), (turn_hi[...], turn_lo[...]))
    squares = coded(shampoo, slab, sent, facts.at[pl.ds(first, count)], 0)
    write(sent, sent_ref.at[pl.ds(first, count), pl.ds(0, data)])

    values = facts[...]
    lane = lax.broadcasted_iota(jnp.int32, values.shape, 2)
    place = 1
    for total in (sums_ref[:8], sums_ref[8:] + squares):
        rest = jnp.sum(total, axis=(0, 1), keepdims=True)
        for _ in range(3):
            piece = rest.astype(BF16)
            rest = rest - piece.astype(F32)
            values = jnp.where(lane == place, piece.reshape(1, 1, 1), values)
            place += 1
    facts[...] = values
    write(facts, sent_ref.at[:, pl.ds(data, TAIL)])
    for copy in writes:
        copy.wait()


def last(side, turn_hi, turn_lo, code, facts, sums, done):
    size, half = turn_hi.shape
    blocks, data, lanes = done.shape
    (start, _), (_, stop) = parts_of(half)[1]
    return pl.pallas_call(
        last_kernel,
        in_specs=[SMEM] + [VMEM] * 6,
        out_specs=HBM,
        out_shape=pltpu.HBM((blocks, data + TAIL, lanes), BF16),
        scratch_shapes=[
            pltpu.VMEM(((stop - start) // 16, data, LANES), BF16),
            pltpu.VMEM(facts.shape, BF16),
            pltpu.SemaphoreType.DMA((4,)),
        ],
        compiler_params=params(16),
        cost_estimate=pl.CostEstimate(
            flops=6 * size * half * (stop - start), bytes_accessed=8 * size * half, transcendentals=0
        ),
    )(side, near(turn_hi), near(turn_lo), near(code), near(facts), near(sums), near(done))


def facts_kernel(got_ref, o_ref):
    depth = got_ref.shape[1]
    o_ref[...] = got_ref[:, depth - TAIL :, :].astype(F32)[:, 0, :]


def facts_of(got):
    blocks, _, lanes = got.shape
    return pl.pallas_call(
        facts_kernel,
        in_specs=[VMEM],
        out_specs=VMEM,
        out_shape=pltpu.VMEM((blocks, lanes), F32),
        compiler_params=params(16),
    )(near(got))


def unpack_kernel(got_ref, o_ref):
    blocks, slab, columns = o_ref.shape
    for tile in range(columns // LANES):
        values = decode(got_ref[:, tile * slab : (tile + 1) * slab, :])
        for block in range(blocks):
            o_ref[block, :, tile * LANES : (tile + 1) * LANES] = values[blocks - 1 - block]


def unpack(got, slab):
    blocks, depth, lanes = got.shape
    return pl.pallas_call(
        unpack_kernel,
        in_specs=[VMEM],
        out_specs=VMEM,
        out_shape=pltpu.VMEM((blocks, slab, (depth - TAIL) // slab * lanes), F32),
        compiler_params=params(16),
        cost_estimate=pl.CostEstimate(
            flops=20 * blocks * depth * lanes, bytes_accessed=8 * blocks * depth * lanes, transcendentals=0
        ),
    )(near(got))


def scale_kernel(entries, values_ref, mine_ref, other_ref, o_ref, scaled, sems):
    blocks = values_ref.shape[0]
    mine = mine_ref[...]
    both = mine + other_ref[...]
    total = lambda k: (both[:, k : k + 1] + both[:, k + 1 : k + 2]) + both[:, k + 2 : k + 3]
    ratio = jnp.sqrt(total(1) / entries + NORM_EPS) / jnp.sqrt(total(4) / entries + NORM_EPS)
    factor = ratio * jnp.exp2(mine[:, 0:1])
    parts = sems.shape[0]
    per = blocks // parts
    writes = []
    for part in range(parts):
        for block in range(part * per, (part + 1) * per):
            source = blocks - 1 - block
            scaled[block] = values_ref[block] * factor[source : source + 1]
        here = pl.ds(part * per, per)
        writes.append(pltpu.make_async_copy(scaled.at[here], o_ref.at[here], sems.at[part]))
        writes[-1].start()
    for write in writes:
        write.wait()


def rescale(values, mine, other, entries):
    def kernel(*refs):
        scale_kernel(entries, *refs)

    return pl.pallas_call(
        kernel,
        in_specs=[VMEM] * 3,
        out_specs=ANY,
        out_shape=jax.ShapeDtypeStruct(values.shape, F32),
        scratch_shapes=[pltpu.VMEM(values.shape, F32), pltpu.SemaphoreType.DMA((4,))],
        compiler_params=params(16),
    )(near(values), mine, other)


def highest(form, left, right):
    return jnp.einsum(form, left, right, precision=lax.Precision.HIGH, preferred_element_type=F32)


def local(grad_partials, second_moment, left_root, right_root, left_stat, right_stat):
    partials = grad_partials[0]
    blocks, slab, size = partials.shape
    half = size // 2
    side = lax.axis_index("dp")

    left = left_root[0]
    early = lax.ppermute(pack(left, 0), "dp", SWAP)

    def deliver(values, left):
        pieces = lax.all_to_all(
            double(values).reshape(2 * blocks, slab, size),
            ("mp", "dp"),
            split_axis=0,
            concat_axis=0,
            tiled=True,
            axis_index_groups=[list(range(2 * blocks))[::-1]],
        )
        return pieces, pack(left, 1)

    def nothing(values, left):
        shapes = jax.eval_shape(lambda: (jnp.zeros((2 * blocks, slab, size), values.dtype), pack(left, 1)))
        return tuple(jnp.zeros(each.shape, each.dtype) for each in shapes)

    pieces, late = lax.cond((side + 2) // 2 == 1, deliver, nothing, partials, left)
    pieces = pieces.reshape(blocks, 2, slab, size)
    late = lax.ppermute(late, "dp", SWAP)
    where = side.astype(jnp.int32).reshape(1)
    grad, moment_new, sent, turn_hi, turn_lo, facts, sums = main(
        where, pieces, second_moment[0], right_root[0], left, early
    )
    sent = last(where, turn_hi, turn_lo, late, facts, sums, sent)
    got = lax.all_to_all(
        sent, "mp", split_axis=0, concat_axis=0, tiled=True, axis_index_groups=[list(range(blocks))[::-1]]
    )
    scale = (1.0 - STAT_DECAY) / size
    rows = lax.dynamic_slice_in_dim(grad, side * half, half, 0)
    columns = lax.dynamic_slice_in_dim(grad, side * half, half, 1)
    left_new = STAT_DECAY * left_stat[0] + scale * highest("ic,jc->ij", rows, grad)
    right_new = STAT_DECAY * right_stat[0] + scale * highest("ri,rj->ij", grad, columns)
    got, left_new, right_new = lax.optimization_barrier((got, left_new, right_new))
    mine = facts_of(got)
    other = lax.ppermute(mine, "dp", SWAP)
    update = rescale(unpack(got, slab), mine, other, float(size * size))
    return (update, moment_new[None], left_new[None], right_new[None])


def solution(mesh):
    return jax.shard_map(
        local,
        mesh=mesh,
        in_specs=(
            P("dp", None, "mp", None),
            P("mp", None, "dp"),
            P("mp", "dp", None),
            P("mp", None, "dp"),
            P("mp", "dp", None),
            P("mp", None, "dp"),
        ),
        out_specs=(
            P(None, "mp", "dp"),
            P("mp", None, "dp"),
            P("mp", "dp", None),
            P("mp", None, "dp"),
        ),
        check_vma=False,
    )
```

```python
import jax
import jax.numpy as jnp
from jax import lax
from jax.experimental import pallas as pl
from jax.experimental.pallas import tpu as pltpu
from jax.sharding import PartitionSpec as P

MOMENT_DECAY = 0.9
STAT_DECAY = 0.9
ADAM_EPS = 1e-08
NORM_EPS = 1e-06
SWAP = [(0, 1), (1, 0)]
TAIL = 16
LANES = 128
POWER = 14
SMALLEST = 1e-30
CHUNKS = 4
EARLY = 9 / 16
F32, BF16 = jnp.float32, jnp.bfloat16


VMEM = pl.BlockSpec(memory_space=pltpu.VMEM)
SMEM = pl.BlockSpec(memory_space=pltpu.SMEM)
ANY = pl.BlockSpec(memory_space=pl.ANY)
HBM = pl.BlockSpec(memory_space=pltpu.HBM)


def params(mebibytes):
    return pltpu.CompilerParams(vmem_limit_bytes=mebibytes * 1024 * 1024)


def near(values):
    return pltpu.with_memory_space_constraint(values, pltpu.VMEM)


def far(values):
    return pltpu.with_memory_space_constraint(values, pltpu.HBM)


def exponent_of(top):
    return jnp.floor(jnp.log2(jnp.maximum(top, SMALLEST))) - 8.0


def encode(scaled):
    square = scaled * scaled
    fourth = square * square
    return (fourth * fourth * fourth * (scaled * jnp.abs(scaled))).astype(BF16)


def decode(coded):
    wide = coded.astype(F32)
    size = jnp.abs(wide)
    root = jnp.exp2(jnp.log2(jnp.maximum(size, 1e-37)) * (1.0 / POWER))
    return jnp.where(size == 0.0, 0.0, jnp.where(wide < 0.0, -root, root))


def split(values):
    high = values.astype(BF16)
    return high, (values - high.astype(F32)).astype(BF16)


def dot3(left, right):
    dot = lambda a, b: jnp.dot(a, b, preferred_element_type=F32)
    return dot(left[0], right[0]) + (dot(left[0], right[1]) + dot(left[1], right[0]))


def fold(values):
    rows, columns = values.shape
    return jnp.sum(values.reshape(rows // 8, 8, columns), axis=0)


def parts_of(rows):
    early = int(rows * EARLY) // 32 * 32
    return ((0, early // 2), (early // 2, early)), ((early, (early + rows) // 2), ((early + rows) // 2, rows))


def pack_kernel(group, left_ref, code_ref, left, sems, others=()):
    depth, columns = left.shape
    origin = group[0][0]
    fetches = []
    for start, stop in group:
        here = pl.ds(start - origin, stop - start)
        source = left_ref.at[pl.ds(start, stop - start)]
        fetches.append(pltpu.make_async_copy(source, left.at[here], sems.at[len(fetches)]))
        fetches[-1].start()
    for other in others:
        other.start()
    tails = []
    for start, stop in group:
        here = slice(start - origin, stop - origin)
        fetches.pop(0).wait()
        values = left[here]
        exponent = exponent_of(jnp.max(jnp.abs(values), axis=(0, 1), keepdims=True))
        code = encode(values * jnp.exp2(-exponent))
        for tile in range(columns // LANES):
            first = tile * depth
            code_ref[first + start - origin : first + stop - origin] = code[
                :, tile * LANES : (tile + 1) * LANES
            ]
        tails.append(jnp.broadcast_to(exponent, (TAIL, LANES)))
    lane = lax.broadcasted_iota(jnp.int32, (TAIL, LANES), 1)
    code_ref[columns // LANES * depth :] = jnp.where(lane < LANES // 2, *tails).astype(BF16)


def front_kernel(group, left_ref, partials_ref, code_ref, turned_ref, left, partials, sems, partial_sems):
    parts = partial_sems.shape[0]
    blocks = partials.shape[0]
    per = blocks // parts
    fetches = []
    for part in range(parts):
        here = pl.ds(part * per, per)
        fetches.append(pltpu.make_async_copy(partials_ref.at[here], partials.at[here], partial_sems.at[part]))
    pack_kernel(group, left_ref, code_ref, left, sems, fetches)
    for part in range(parts):
        fetches[part].wait()
        for block in range(part * per, (part + 1) * per):
            turned_ref[blocks - 1 - block] = partials[block]


def front(left, partials):
    columns = left.shape[1]
    group = parts_of(left.shape[0])[0]
    depth = group[1][1] - group[0][0]

    def kernel(*refs):
        front_kernel(group, *refs)

    return pl.pallas_call(
        kernel,
        in_specs=[HBM, HBM],
        out_specs=[VMEM, VMEM],
        out_shape=[
            jax.ShapeDtypeStruct((columns // LANES * depth + TAIL, LANES), BF16),
            pltpu.VMEM(partials.shape, BF16),
        ],
        scratch_shapes=[
            pltpu.VMEM((depth, columns), F32),
            pltpu.VMEM(partials.shape, BF16),
            pltpu.SemaphoreType.DMA((2,)),
            pltpu.SemaphoreType.DMA((2,)),
        ],
        compiler_params=params(16),
    )(far(left), far(partials))


def pack(left, which):
    columns = left.shape[1]
    group = parts_of(left.shape[0])[which]
    depth = group[1][1] - group[0][0]

    def kernel(*refs):
        pack_kernel(group, *refs)

    return pl.pallas_call(
        kernel,
        in_specs=[HBM],
        out_specs=VMEM,
        out_shape=jax.ShapeDtypeStruct((columns // LANES * depth + TAIL, LANES), BF16),
        scratch_shapes=[pltpu.VMEM((depth, columns), F32), pltpu.SemaphoreType.DMA((2,))],
        compiler_params=params(16),
    )(far(left))


def root_of(code_ref, group):
    origin, end = group[0][0], group[1][1]
    depth = end - origin
    tiles = (code_ref.shape[0] - TAIL) // depth
    scales = jnp.exp2(code_ref[tiles * depth :].astype(F32)[0:1])
    rows = []
    for part, (start, stop) in enumerate(group):
        lane = part * (LANES // 2)
        columns = [
            decode(code_ref[tile * depth + start - origin : tile * depth + stop - origin])
            for tile in range(tiles)
        ]
        rows.append(jnp.concatenate(columns, axis=1) * scales[:, lane : lane + 1])
    return jnp.concatenate(rows, axis=0)


def double_kernel(turned_ref, doubled_ref, sems):
    writes = []
    for copy in range(2):
        writes.append(pltpu.make_async_copy(turned_ref, doubled_ref.at[:, copy], sems.at[copy]))
        writes[-1].start()
    for write in writes:
        write.wait()


def double(turned):
    blocks, slab, size = turned.shape
    return pl.pallas_call(
        double_kernel,
        in_specs=[VMEM],
        out_specs=HBM,
        out_shape=pltpu.HBM((blocks, 2, slab, size), BF16),
        scratch_shapes=[pltpu.SemaphoreType.DMA((2,))],
        compiler_params=params(16),
    )(near(turned))


def coded(shampoo, slab, sent, facts, first):
    rows, half = shampoo.shape
    messages = rows // slab
    grouped = shampoo.reshape(messages, slab, half)
    exponent = exponent_of(jnp.max(jnp.abs(grouped), axis=(1, 2), keepdims=True))
    code = encode(grouped * jnp.exp2(-exponent))
    wide = jnp.broadcast_to(exponent, (messages, TAIL, LANES)).astype(BF16)
    for message in range(messages):
        place = first + (messages - 1 - message)
        for tile in range(half // LANES):
            sent[place, tile * slab : (tile + 1) * slab, :] = code[
                message, :, tile * LANES : (tile + 1) * LANES
            ]
        facts[place] = wide[message]
    return fold(shampoo * shampoo)


def main_kernel(
    side_ref, right_ref, pieces_ref, moment_ref, left_ref, code_ref,
    grad_ref, new_ref, sent, turn_hi, turn_lo, facts_ref, sums_ref,
    pieces, moment, left, grad, new, right_hi, right_lo, fetch_sems, write_sems,
):
    side = side_ref[0]
    blocks, _, slab, size = pieces.shape
    half = size // 2
    chunks = CHUNKS
    rows = size // chunks
    messages = rows // slab
    early = parts_of(half)[0]

    def fetch(source, target, slot):
        copy = pltpu.make_async_copy(source, target, fetch_sems.at[slot])
        copy.start()
        return copy

    def fetch_pieces(chunk):
        here = pl.ds(blocks - (chunk + 1) * messages, messages)
        return fetch(pieces_ref.at[here], pieces.at[here], chunk)

    def fetch_moment(chunk):
        here = pl.ds(chunk * rows, rows)
        return fetch(moment_ref.at[here], moment.at[here], chunks + chunk)

    piece_arrivals = [fetch_pieces(chunk) for chunk in range(chunks)]
    moment_arrivals = [fetch_moment(chunk) for chunk in range(chunks)]
    writes = []

    def write(source, target):
        writes.append(pltpu.make_async_copy(source, target, write_sems.at[len(writes)]))
        writes[-1].start()

    right_hi[...], right_lo[...] = split(right_ref[...])
    adam = jnp.zeros((8, half), F32)
    for chunk in range(chunks):
        here = slice(chunk * rows, (chunk + 1) * rows)
        piece_arrivals[chunk].wait()
        if chunk == 0:
            left_arrival = fetch(left_ref, left, 2 * chunks)
        for message in range(messages):
            source = chunk * messages + message
            piece = blocks - 1 - source
            grad[source * slab : (source + 1) * slab] = pieces[piece, 0].astype(F32) + pieces[
                piece, 1
            ].astype(F32)
        write(grad.at[pl.ds(chunk * rows, rows)], grad_ref.at[pl.ds(chunk * rows, rows)])
        turned = dot3(split(grad[here]), (right_hi[...], right_lo[...]))
        turn_hi[here], turn_lo[here] = split(turned)
        mine = grad[here, pl.ds(pl.multiple_of(side * half, half), half)]
        moment_arrivals[chunk].wait()
        moment_new = MOMENT_DECAY * moment[here] + (1.0 - MOMENT_DECAY) * mine * mine
        new[here] = moment_new
        direction = mine / (jnp.sqrt(moment_new) + ADAM_EPS)
        adam += fold(direction * direction)
    write(new, new_ref)

    def finish(left, row_block):
        shampoo = dot3(split(left), (turn_hi[...], turn_lo[...]))
        count = left.shape[0] // slab
        first = blocks - count - row_block
        return coded(shampoo, slab, sent, facts_ref, first)

    squares = jnp.zeros((8, half), F32)
    left_arrival.wait()
    for start in range(0, half, rows):
        squares += finish(left[start : start + rows], side * (blocks // 2) + start // slab)
    squares += finish(root_of(code_ref, early), (1 - side) * (blocks // 2))
    sums_ref[:8] = adam
    sums_ref[8:] = squares
    for copy in writes:
        copy.wait()


def main(side, pieces, moment, right, left, code):
    size, half = right.shape
    blocks, _, slab, _ = pieces.shape
    data = half // LANES * slab
    return pl.pallas_call(
        main_kernel,
        in_specs=[SMEM, VMEM, HBM, HBM, HBM, VMEM],
        out_specs=[HBM, ANY, VMEM, VMEM, VMEM, VMEM, VMEM],
        out_shape=[
            pltpu.HBM((size, size), F32),
            jax.ShapeDtypeStruct((size, half), F32),
            pltpu.VMEM((blocks, data, LANES), BF16),
            pltpu.VMEM((size, half), BF16),
            pltpu.VMEM((size, half), BF16),
            pltpu.VMEM((blocks, TAIL, LANES), BF16),
            pltpu.VMEM((16, half), F32),
        ],
        scratch_shapes=[
            pltpu.VMEM(pieces.shape, BF16),
            pltpu.VMEM(moment.shape, F32),
            pltpu.VMEM(left.shape, F32),
            pltpu.VMEM((size, size), F32),
            pltpu.VMEM(moment.shape, F32),
            pltpu.VMEM((size, half), BF16),
            pltpu.VMEM((size, half), BF16),
            pltpu.SemaphoreType.DMA((2 * CHUNKS + 1,)),
            pltpu.SemaphoreType.DMA((CHUNKS + 1,)),
        ],
        compiler_params=params(36),
        cost_estimate=pl.CostEstimate(
            flops=12 * size * size * half, bytes_accessed=16 * size * size, transcendentals=4 * size * half
        ),
    )(side, near(right), far(pieces), far(moment), far(left), near(code))


def last_kernel(side_ref, turn_hi, turn_lo, code_ref, facts_ref, sums_ref, done_ref, sent_ref, sent, facts, sems):
    side = side_ref[0]
    blocks = facts.shape[0]
    slab = 16
    data = sent.shape[1]
    half = turn_hi.shape[1]
    late = parts_of(half)[1]
    count = sent.shape[0]
    row_block = (1 - side) * (blocks // 2) + late[0][0] // slab
    first = blocks - count - row_block

    writes = []

    def write(source, target):
        writes.append(pltpu.make_async_copy(source, target, sems.at[len(writes)]))
        writes[-1].start()

    rest = blocks // 2 - count
    for start, extent in (((1 - side) * (blocks // 2), blocks // 2), (first + count, rest)):
        here = pl.ds(start, extent)
        write(done_ref.at[here], sent_ref.at[here, pl.ds(0, data)])
    facts[...] = facts_ref[...]
    shampoo = dot3(split(root_of(code_ref, late)), (turn_hi[...], turn_lo[...]))
    squares = coded(shampoo, slab, sent, facts.at[pl.ds(first, count)], 0)
    write(sent, sent_ref.at[pl.ds(first, count), pl.ds(0, data)])

    values = facts[...]
    lane = lax.broadcasted_iota(jnp.int32, values.shape, 2)
    place = 1
    for total in (sums_ref[:8], sums_ref[8:] + squares):
        rest = jnp.sum(total, axis=(0, 1), keepdims=True)
        for _ in range(3):
            piece = rest.astype(BF16)
            rest = rest - piece.astype(F32)
            values = jnp.where(lane == place, piece.reshape(1, 1, 1), values)
            place += 1
    facts[...] = values
    write(facts, sent_ref.at[:, pl.ds(data, TAIL)])
    for copy in writes:
        copy.wait()


def last(side, turn_hi, turn_lo, code, facts, sums, done):
    size, half = turn_hi.shape
    blocks, data, lanes = done.shape
    (start, _), (_, stop) = parts_of(half)[1]
    return pl.pallas_call(
        last_kernel,
        in_specs=[SMEM] + [VMEM] * 6,
        out_specs=HBM,
        out_shape=pltpu.HBM((blocks, data + TAIL, lanes), BF16),
        scratch_shapes=[
            pltpu.VMEM(((stop - start) // 16, data, LANES), BF16),
            pltpu.VMEM(facts.shape, BF16),
            pltpu.SemaphoreType.DMA((4,)),
        ],
        compiler_params=params(16),
        cost_estimate=pl.CostEstimate(
            flops=6 * size * half * (stop - start), bytes_accessed=8 * size * half, transcendentals=0
        ),
    )(side, near(turn_hi), near(turn_lo), near(code), near(facts), near(sums), near(done))


def facts_kernel(got_ref, o_ref):
    depth = got_ref.shape[1]
    o_ref[...] = got_ref[:, depth - TAIL :, :].astype(F32)[:, 0, :]


def facts_of(got):
    blocks, _, lanes = got.shape
    return pl.pallas_call(
        facts_kernel,
        in_specs=[VMEM],
        out_specs=VMEM,
        out_shape=pltpu.VMEM((blocks, lanes), F32),
        compiler_params=params(16),
    )(near(got))


def unpack_kernel(got_ref, o_ref):
    blocks, slab, columns = o_ref.shape
    for tile in range(columns // LANES):
        values = decode(got_ref[:, tile * slab : (tile + 1) * slab, :])
        for block in range(blocks):
            o_ref[block, :, tile * LANES : (tile + 1) * LANES] = values[blocks - 1 - block]


def unpack(got, slab):
    blocks, depth, lanes = got.shape
    return pl.pallas_call(
        unpack_kernel,
        in_specs=[VMEM],
        out_specs=VMEM,
        out_shape=pltpu.VMEM((blocks, slab, (depth - TAIL) // slab * lanes), F32),
        compiler_params=params(16),
        cost_estimate=pl.CostEstimate(
            flops=20 * blocks * depth * lanes, bytes_accessed=8 * blocks * depth * lanes, transcendentals=0
        ),
    )(near(got))


def scale_kernel(entries, values_ref, mine_ref, other_ref, o_ref, scaled, sems):
    blocks = values_ref.shape[0]
    mine = mine_ref[...]
    both = mine + other_ref[...]
    total = lambda k: (both[:, k : k + 1] + both[:, k + 1 : k + 2]) + both[:, k + 2 : k + 3]
    ratio = jnp.sqrt(total(1) / entries + NORM_EPS) / jnp.sqrt(total(4) / entries + NORM_EPS)
    factor = ratio * jnp.exp2(mine[:, 0:1])
    parts = sems.shape[0]
    per = blocks // parts
    writes = []
    for part in range(parts):
        for block in range(part * per, (part + 1) * per):
            source = blocks - 1 - block
            scaled[block] = values_ref[block] * factor[source : source + 1]
        here = pl.ds(part * per, per)
        writes.append(pltpu.make_async_copy(scaled.at[here], o_ref.at[here], sems.at[part]))
        writes[-1].start()
    for write in writes:
        write.wait()


def rescale(values, mine, other, entries):
    def kernel(*refs):
        scale_kernel(entries, *refs)

    return pl.pallas_call(
        kernel,
        in_specs=[VMEM] * 3,
        out_specs=ANY,
        out_shape=jax.ShapeDtypeStruct(values.shape, F32),
        scratch_shapes=[pltpu.VMEM(values.shape, F32), pltpu.SemaphoreType.DMA((4,))],
        compiler_params=params(16),
    )(near(values), mine, other)


def highest(form, left, right):
    return jnp.einsum(form, left, right, precision=lax.Precision.HIGH, preferred_element_type=F32)


def local(grad_partials, second_moment, left_root, right_root, left_stat, right_stat):
    partials = grad_partials[0]
    blocks, slab, size = partials.shape
    half = size // 2
    side = lax.axis_index("dp")

    left = left_root[0]
    early, turned = front(left, partials)
    early = lax.ppermute(early, "dp", SWAP)

    def deliver(values, left):
        pieces = lax.all_to_all(
            values.reshape(2 * blocks, slab, size),
            ("mp", "dp"),
            split_axis=0,
            concat_axis=0,
            tiled=True,
            axis_index_groups=[list(range(2 * blocks))[::-1]],
        )
        return pieces, pack(left, 1)

    def nothing(values, left):
        shapes = jax.eval_shape(lambda: (jnp.zeros((2 * blocks, slab, size), values.dtype), pack(left, 1)))
        return tuple(jnp.zeros(each.shape, each.dtype) for each in shapes)

    pieces, late = lax.cond((side + 2) // 2 == 1, deliver, nothing, double(turned), left)
    pieces = pieces.reshape(blocks, 2, slab, size)
    late = lax.ppermute(late, "dp", SWAP)
    where = side.astype(jnp.int32).reshape(1)
    grad, moment_new, sent, turn_hi, turn_lo, facts, sums = main(
        where, pieces, second_moment[0], right_root[0], left, early
    )
    sent = last(where, turn_hi, turn_lo, late, facts, sums, sent)
    got = lax.all_to_all(
        sent, "mp", split_axis=0, concat_axis=0, tiled=True, axis_index_groups=[list(range(blocks))[::-1]]
    )
    scale = (1.0 - STAT_DECAY) / size
    rows = lax.dynamic_slice_in_dim(grad, side * half, half, 0)
    columns = lax.dynamic_slice_in_dim(grad, side * half, half, 1)
    left_new = STAT_DECAY * left_stat[0] + scale * highest("ic,jc->ij", rows, grad)
    right_new = STAT_DECAY * right_stat[0] + scale * highest("ri,rj->ij", grad, columns)
    got, left_new, right_new = lax.optimization_barrier((got, left_new, right_new))
    mine = facts_of(got)
    other = lax.ppermute(mine, "dp", SWAP)
    update = rescale(unpack(got, slab), mine, other, float(size * size))
    return (update, moment_new[None], left_new[None], right_new[None])


def solution(mesh):
    return jax.shard_map(
        local,
        mesh=mesh,
        in_specs=(
            P("dp", None, "mp", None),
            P("mp", None, "dp"),
            P("mp", "dp", None),
            P("mp", None, "dp"),
            P("mp", "dp", None),
            P("mp", None, "dp"),
        ),
        out_specs=(
            P(None, "mp", "dp"),
            P("mp", None, "dp"),
            P("mp", "dp", None),
            P("mp", None, "dp"),
        ),
        check_vma=False,
    )
```

```python
import jax
import jax.numpy as jnp
from jax import lax
from jax.experimental import pallas as pl
from jax.experimental.pallas import tpu as pltpu
from jax.sharding import PartitionSpec as P

MOMENT_DECAY = 0.9
STAT_DECAY = 0.9
ADAM_EPS = 1e-08
NORM_EPS = 1e-06
SWAP = [(0, 1), (1, 0)]
TAIL = 16
LANES = 128
POWER = 14
SMALLEST = 1e-30
CHUNKS = 4
EARLY = 9 / 16
F32, BF16 = jnp.float32, jnp.bfloat16


VMEM = pl.BlockSpec(memory_space=pltpu.VMEM)
SMEM = pl.BlockSpec(memory_space=pltpu.SMEM)
ANY = pl.BlockSpec(memory_space=pl.ANY)
HBM = pl.BlockSpec(memory_space=pltpu.HBM)


def params(mebibytes):
    return pltpu.CompilerParams(vmem_limit_bytes=mebibytes * 1024 * 1024)


def near(values):
    return pltpu.with_memory_space_constraint(values, pltpu.VMEM)


def far(values):
    return pltpu.with_memory_space_constraint(values, pltpu.HBM)


def exponent_of(top):
    return jnp.floor(jnp.log2(jnp.maximum(top, SMALLEST))) - 8.0


def encode(scaled):
    square = scaled * scaled
    fourth = square * square
    return (fourth * fourth * fourth * (scaled * jnp.abs(scaled))).astype(BF16)


def decode(coded):
    wide = coded.astype(F32)
    size = jnp.abs(wide)
    root = jnp.exp2(jnp.log2(jnp.maximum(size, 1e-37)) * (1.0 / POWER))
    return jnp.where(size == 0.0, 0.0, jnp.where(wide < 0.0, -root, root))


def split(values):
    high = values.astype(BF16)
    return high, (values - high.astype(F32)).astype(BF16)


def dot3(left, right):
    dot = lambda a, b: jnp.dot(a, b, preferred_element_type=F32)
    return dot(left[0], right[0]) + (dot(left[0], right[1]) + dot(left[1], right[0]))


def fold(values):
    rows, columns = values.shape
    return jnp.sum(values.reshape(rows // 8, 8, columns), axis=0)


def parts_of(rows):
    early = int(rows * EARLY) // 32 * 32
    return ((0, early // 2), (early // 2, early)), ((early, (early + rows) // 2), ((early + rows) // 2, rows))


def pack_kernel(group, left_ref, code_ref, left, sems, others=()):
    depth, columns = left.shape
    origin = group[0][0]
    fetches = []
    for start, stop in group:
        here = pl.ds(start - origin, stop - start)
        source = left_ref.at[pl.ds(start, stop - start)]
        fetches.append(pltpu.make_async_copy(source, left.at[here], sems.at[len(fetches)]))
        fetches[-1].start()
    for other in others:
        other.start()
    tails = []
    for start, stop in group:
        here = slice(start - origin, stop - origin)
        fetches.pop(0).wait()
        values = left[here]
        exponent = exponent_of(jnp.max(jnp.abs(values), axis=(0, 1), keepdims=True))
        code = encode(values * jnp.exp2(-exponent))
        for tile in range(columns // LANES):
            first = tile * depth
            code_ref[first + start - origin : first + stop - origin] = code[
                :, tile * LANES : (tile + 1) * LANES
            ]
        tails.append(jnp.broadcast_to(exponent, (TAIL, LANES)))
    lane = lax.broadcasted_iota(jnp.int32, (TAIL, LANES), 1)
    code_ref[columns // LANES * depth :] = jnp.where(lane < LANES // 2, *tails).astype(BF16)


def front_kernel(group, left_ref, partials_ref, code_ref, turned_ref, left, partials, sems, partial_sems):
    parts = partial_sems.shape[0]
    blocks = partials.shape[0]
    per = blocks // parts
    fetches = []
    for part in range(parts):
        here = pl.ds(part * per, per)
        fetches.append(pltpu.make_async_copy(partials_ref.at[here], partials.at[here], partial_sems.at[part]))
    pack_kernel(group, left_ref, code_ref, left, sems, fetches)
    for part in range(parts):
        fetches[part].wait()
        for block in range(part * per, (part + 1) * per):
            turned_ref[blocks - 1 - block] = partials[block]


def front(left, partials):
    columns = left.shape[1]
    group = parts_of(left.shape[0])[0]
    depth = group[1][1] - group[0][0]

    def kernel(*refs):
        front_kernel(group, *refs)

    return pl.pallas_call(
        kernel,
        in_specs=[HBM, HBM],
        out_specs=[VMEM, VMEM],
        out_shape=[
            jax.ShapeDtypeStruct((columns // LANES * depth + TAIL, LANES), BF16),
            pltpu.VMEM(partials.shape, BF16),
        ],
        scratch_shapes=[
            pltpu.VMEM((depth, columns), F32),
            pltpu.VMEM(partials.shape, BF16),
            pltpu.SemaphoreType.DMA((2,)),
            pltpu.SemaphoreType.DMA((2,)),
        ],
        compiler_params=params(16),
    )(far(left), far(partials))


def pack(left, which):
    columns = left.shape[1]
    group = parts_of(left.shape[0])[which]
    depth = group[1][1] - group[0][0]

    def kernel(*refs):
        pack_kernel(group, *refs)

    return pl.pallas_call(
        kernel,
        in_specs=[HBM],
        out_specs=VMEM,
        out_shape=jax.ShapeDtypeStruct((columns // LANES * depth + TAIL, LANES), BF16),
        scratch_shapes=[pltpu.VMEM((depth, columns), F32), pltpu.SemaphoreType.DMA((2,))],
        compiler_params=params(16),
    )(far(left))


def root_of(code_ref, group):
    origin, end = group[0][0], group[1][1]
    depth = end - origin
    tiles = (code_ref.shape[0] - TAIL) // depth
    scales = jnp.exp2(code_ref[tiles * depth :].astype(F32)[0:1])
    rows = []
    for part, (start, stop) in enumerate(group):
        lane = part * (LANES // 2)
        columns = [
            decode(code_ref[tile * depth + start - origin : tile * depth + stop - origin])
            for tile in range(tiles)
        ]
        rows.append(jnp.concatenate(columns, axis=1) * scales[:, lane : lane + 1])
    return jnp.concatenate(rows, axis=0)


def double_kernel(turned_ref, doubled_ref, sems):
    writes = []
    for copy in range(2):
        writes.append(pltpu.make_async_copy(turned_ref, doubled_ref.at[:, copy], sems.at[copy]))
        writes[-1].start()
    for write in writes:
        write.wait()


def double(turned):
    blocks, slab, size = turned.shape
    return pl.pallas_call(
        double_kernel,
        in_specs=[VMEM],
        out_specs=HBM,
        out_shape=pltpu.HBM((blocks, 2, slab, size), BF16),
        scratch_shapes=[pltpu.SemaphoreType.DMA((2,))],
        compiler_params=params(16),
    )(near(turned))


def coded(shampoo, slab, sent, facts, first):
    rows, half = shampoo.shape
    messages = rows // slab
    grouped = shampoo.reshape(messages, slab, half)
    exponent = exponent_of(jnp.max(jnp.abs(grouped), axis=(1, 2), keepdims=True))
    code = encode(grouped * jnp.exp2(-exponent))
    wide = jnp.broadcast_to(exponent, (messages, TAIL, LANES)).astype(BF16)
    for message in range(messages):
        place = first + (messages - 1 - message)
        for tile in range(half // LANES):
            sent[place, tile * slab : (tile + 1) * slab, :] = code[
                message, :, tile * LANES : (tile + 1) * LANES
            ]
        facts[place] = wide[message]
    return fold(shampoo * shampoo)


def main_kernel(
    side_ref, right_ref, pieces_ref, moment_ref, left_ref, code_ref,
    grad_ref, new_ref, sent, turn_hi, turn_lo, facts_ref, sums_ref,
    pieces, moment, left, grad, new, right_hi, right_lo, fetch_sems, write_sems,
):
    side = side_ref[0]
    blocks, _, slab, size = pieces.shape
    half = size // 2
    chunks = CHUNKS
    rows = size // chunks
    messages = rows // slab
    early = parts_of(half)[0]

    def fetch(source, target, slot):
        copy = pltpu.make_async_copy(source, target, fetch_sems.at[slot])
        copy.start()
        return copy

    def fetch_pieces(chunk):
        here = pl.ds(blocks - (chunk + 1) * messages, messages)
        return fetch(pieces_ref.at[here], pieces.at[here], chunk)

    def fetch_moment(chunk):
        here = pl.ds(chunk * rows, rows)
        return fetch(moment_ref.at[here], moment.at[here], chunks + chunk)

    piece_arrivals = [fetch_pieces(chunk) for chunk in range(chunks)]
    moment_arrivals = [fetch_moment(chunk) for chunk in range(chunks)]
    writes = []

    def write(source, target):
        writes.append(pltpu.make_async_copy(source, target, write_sems.at[len(writes)]))
        writes[-1].start()

    right_hi[...], right_lo[...] = split(right_ref[...])
    adam = jnp.zeros((8, half), F32)
    for chunk in range(chunks):
        here = slice(chunk * rows, (chunk + 1) * rows)
        piece_arrivals[chunk].wait()
        if chunk == 0:
            left_arrival = fetch(left_ref, left, 2 * chunks)
        for message in range(messages):
            source = chunk * messages + message
            piece = blocks - 1 - source
            grad[source * slab : (source + 1) * slab] = pieces[piece, 0].astype(F32) + pieces[
                piece, 1
            ].astype(F32)
        write(grad.at[pl.ds(chunk * rows, rows)], grad_ref.at[pl.ds(chunk * rows, rows)])
        turned = dot3(split(grad[here]), (right_hi[...], right_lo[...]))
        turn_hi[here], turn_lo[here] = split(turned)
        mine = grad[here, pl.ds(pl.multiple_of(side * half, half), half)]
        moment_arrivals[chunk].wait()
        moment_new = MOMENT_DECAY * moment[here] + (1.0 - MOMENT_DECAY) * mine * mine
        new[here] = moment_new
        direction = mine / (moment_new * lax.rsqrt(moment_new) + ADAM_EPS)
        adam += fold(direction * direction)
    write(new, new_ref)

    def finish(left, row_block):
        shampoo = dot3(split(left), (turn_hi[...], turn_lo[...]))
        count = left.shape[0] // slab
        first = blocks - count - row_block
        return coded(shampoo, slab, sent, facts_ref, first)

    squares = jnp.zeros((8, half), F32)
    left_arrival.wait()
    for start in range(0, half, rows):
        squares += finish(left[start : start + rows], side * (blocks // 2) + start // slab)
    squares += finish(root_of(code_ref, early), (1 - side) * (blocks // 2))
    sums_ref[:8] = adam
    sums_ref[8:] = squares
    for copy in writes:
        copy.wait()


def main(side, pieces, moment, right, left, code):
    size, half = right.shape
    blocks, _, slab, _ = pieces.shape
    data = half // LANES * slab
    return pl.pallas_call(
        main_kernel,
        in_specs=[SMEM, VMEM, HBM, HBM, HBM, VMEM],
        out_specs=[HBM, ANY, VMEM, VMEM, VMEM, VMEM, VMEM],
        out_shape=[
            pltpu.HBM((size, size), F32),
            jax.ShapeDtypeStruct((size, half), F32),
            pltpu.VMEM((blocks, data, LANES), BF16),
            pltpu.VMEM((size, half), BF16),
            pltpu.VMEM((size, half), BF16),
            pltpu.VMEM((blocks, TAIL, LANES), BF16),
            pltpu.VMEM((16, half), F32),
        ],
        scratch_shapes=[
            pltpu.VMEM(pieces.shape, BF16),
            pltpu.VMEM(moment.shape, F32),
            pltpu.VMEM(left.shape, F32),
            pltpu.VMEM((size, size), F32),
            pltpu.VMEM(moment.shape, F32),
            pltpu.VMEM((size, half), BF16),
            pltpu.VMEM((size, half), BF16),
            pltpu.SemaphoreType.DMA((2 * CHUNKS + 1,)),
            pltpu.SemaphoreType.DMA((CHUNKS + 1,)),
        ],
        compiler_params=params(36),
        cost_estimate=pl.CostEstimate(
            flops=12 * size * size * half, bytes_accessed=16 * size * size, transcendentals=4 * size * half
        ),
    )(side, near(right), far(pieces), far(moment), far(left), near(code))


def last_kernel(side_ref, turn_hi, turn_lo, code_ref, facts_ref, sums_ref, done_ref, sent_ref, sent, facts, sems):
    side = side_ref[0]
    blocks = facts.shape[0]
    slab = 16
    data = sent.shape[1]
    half = turn_hi.shape[1]
    late = parts_of(half)[1]
    count = sent.shape[0]
    row_block = (1 - side) * (blocks // 2) + late[0][0] // slab
    first = blocks - count - row_block

    writes = []

    def write(source, target):
        writes.append(pltpu.make_async_copy(source, target, sems.at[len(writes)]))
        writes[-1].start()

    rest = blocks // 2 - count
    for start, extent in (((1 - side) * (blocks // 2), blocks // 2), (first + count, rest)):
        here = pl.ds(start, extent)
        write(done_ref.at[here], sent_ref.at[here, pl.ds(0, data)])
    facts[...] = facts_ref[...]
    shampoo = dot3(split(root_of(code_ref, late)), (turn_hi[...], turn_lo[...]))
    squares = coded(shampoo, slab, sent, facts.at[pl.ds(first, count)], 0)
    write(sent, sent_ref.at[pl.ds(first, count), pl.ds(0, data)])

    values = facts[...]
    lane = lax.broadcasted_iota(jnp.int32, values.shape, 2)
    place = 1
    for total in (sums_ref[:8], sums_ref[8:] + squares):
        rest = jnp.sum(total, axis=(0, 1), keepdims=True)
        for _ in range(3):
            piece = rest.astype(BF16)
            rest = rest - piece.astype(F32)
            values = jnp.where(lane == place, piece.reshape(1, 1, 1), values)
            place += 1
    facts[...] = values
    write(facts, sent_ref.at[:, pl.ds(data, TAIL)])
    for copy in writes:
        copy.wait()


def last(side, turn_hi, turn_lo, code, facts, sums, done):
    size, half = turn_hi.shape
    blocks, data, lanes = done.shape
    (start, _), (_, stop) = parts_of(half)[1]
    return pl.pallas_call(
        last_kernel,
        in_specs=[SMEM] + [VMEM] * 6,
        out_specs=HBM,
        out_shape=pltpu.HBM((blocks, data + TAIL, lanes), BF16),
        scratch_shapes=[
            pltpu.VMEM(((stop - start) // 16, data, LANES), BF16),
            pltpu.VMEM(facts.shape, BF16),
            pltpu.SemaphoreType.DMA((4,)),
        ],
        compiler_params=params(16),
        cost_estimate=pl.CostEstimate(
            flops=6 * size * half * (stop - start), bytes_accessed=8 * size * half, transcendentals=0
        ),
    )(side, near(turn_hi), near(turn_lo), near(code), near(facts), near(sums), near(done))


def facts_kernel(got_ref, o_ref):
    depth = got_ref.shape[1]
    o_ref[...] = got_ref[:, depth - TAIL :, :].astype(F32)[:, 0, :]


def facts_of(got):
    blocks, _, lanes = got.shape
    return pl.pallas_call(
        facts_kernel,
        in_specs=[VMEM],
        out_specs=VMEM,
        out_shape=pltpu.VMEM((blocks, lanes), F32),
        compiler_params=params(16),
    )(near(got))


def unpack_kernel(got_ref, o_ref):
    blocks, slab, columns = o_ref.shape
    for tile in range(columns // LANES):
        values = decode(got_ref[:, tile * slab : (tile + 1) * slab, :])
        for block in range(blocks):
            o_ref[block, :, tile * LANES : (tile + 1) * LANES] = values[blocks - 1 - block]


def unpack(got, slab):
    blocks, depth, lanes = got.shape
    return pl.pallas_call(
        unpack_kernel,
        in_specs=[VMEM],
        out_specs=VMEM,
        out_shape=pltpu.VMEM((blocks, slab, (depth - TAIL) // slab * lanes), F32),
        compiler_params=params(16),
        cost_estimate=pl.CostEstimate(
            flops=20 * blocks * depth * lanes, bytes_accessed=8 * blocks * depth * lanes, transcendentals=0
        ),
    )(near(got))


def scale_kernel(entries, values_ref, mine_ref, other_ref, o_ref, scaled, sems):
    blocks = values_ref.shape[0]
    mine = mine_ref[...]
    both = mine + other_ref[...]
    total = lambda k: (both[:, k : k + 1] + both[:, k + 1 : k + 2]) + both[:, k + 2 : k + 3]
    ratio = jnp.sqrt(total(1) / entries + NORM_EPS) / jnp.sqrt(total(4) / entries + NORM_EPS)
    factor = ratio * jnp.exp2(mine[:, 0:1])
    parts = sems.shape[0]
    per = blocks // parts
    writes = []
    for part in range(parts):
        for block in range(part * per, (part + 1) * per):
            source = blocks - 1 - block
            scaled[block] = values_ref[block] * factor[source : source + 1]
        here = pl.ds(part * per, per)
        writes.append(pltpu.make_async_copy(scaled.at[here], o_ref.at[here], sems.at[part]))
        writes[-1].start()
    for write in writes:
        write.wait()


def rescale(values, mine, other, entries):
    def kernel(*refs):
        scale_kernel(entries, *refs)

    return pl.pallas_call(
        kernel,
        in_specs=[VMEM] * 3,
        out_specs=ANY,
        out_shape=jax.ShapeDtypeStruct(values.shape, F32),
        scratch_shapes=[pltpu.VMEM(values.shape, F32), pltpu.SemaphoreType.DMA((4,))],
        compiler_params=params(16),
    )(near(values), mine, other)


def highest(form, left, right):
    return jnp.einsum(form, left, right, precision=lax.Precision.HIGH, preferred_element_type=F32)


def local(grad_partials, second_moment, left_root, right_root, left_stat, right_stat):
    partials = grad_partials[0]
    blocks, slab, size = partials.shape
    half = size // 2
    side = lax.axis_index("dp")

    left = left_root[0]
    early, turned = front(left, partials)
    early = lax.ppermute(early, "dp", SWAP)

    def deliver(values, left):
        pieces = lax.all_to_all(
            values.reshape(2 * blocks, slab, size),
            ("mp", "dp"),
            split_axis=0,
            concat_axis=0,
            tiled=True,
            axis_index_groups=[list(range(2 * blocks))[::-1]],
        )
        return pieces, pack(left, 1)

    def nothing(values, left):
        shapes = jax.eval_shape(lambda: (jnp.zeros((2 * blocks, slab, size), values.dtype), pack(left, 1)))
        return tuple(jnp.zeros(each.shape, each.dtype) for each in shapes)

    pieces, late = lax.cond((side + 2) // 2 == 1, deliver, nothing, double(turned), left)
    pieces = pieces.reshape(blocks, 2, slab, size)
    late = lax.ppermute(late, "dp", SWAP)
    where = side.astype(jnp.int32).reshape(1)
    grad, moment_new, sent, turn_hi, turn_lo, facts, sums = main(
        where, pieces, second_moment[0], right_root[0], left, early
    )
    sent = last(where, turn_hi, turn_lo, late, facts, sums, sent)
    got = lax.all_to_all(
        sent, "mp", split_axis=0, concat_axis=0, tiled=True, axis_index_groups=[list(range(blocks))[::-1]]
    )
    scale = (1.0 - STAT_DECAY) / size
    rows = lax.dynamic_slice_in_dim(grad, side * half, half, 0)
    columns = lax.dynamic_slice_in_dim(grad, side * half, half, 1)
    left_new = STAT_DECAY * left_stat[0] + scale * highest("ic,jc->ij", rows, grad)
    right_new = STAT_DECAY * right_stat[0] + scale * highest("ri,rj->ij", grad, columns)
    got, left_new, right_new = lax.optimization_barrier((got, left_new, right_new))
    mine = facts_of(got)
    other = lax.ppermute(mine, "dp", SWAP)
    update = rescale(unpack(got, slab), mine, other, float(size * size))
    return (update, moment_new[None], left_new[None], right_new[None])


def solution(mesh):
    return jax.shard_map(
        local,
        mesh=mesh,
        in_specs=(
            P("dp", None, "mp", None),
            P("mp", None, "dp"),
            P("mp", "dp", None),
            P("mp", None, "dp"),
            P("mp", "dp", None),
            P("mp", None, "dp"),
        ),
        out_specs=(
            P(None, "mp", "dp"),
            P("mp", None, "dp"),
            P("mp", "dp", None),
            P("mp", None, "dp"),
        ),
        check_vma=False,
    )
```

```python
import jax
import jax.numpy as jnp
from jax import lax
from jax.experimental import pallas as pl
from jax.experimental.pallas import tpu as pltpu
from jax.sharding import PartitionSpec as P

MOMENT_DECAY = 0.9
STAT_DECAY = 0.9
ADAM_EPS = 1e-08
NORM_EPS = 1e-06
SWAP = [(0, 1), (1, 0)]
TAIL = 16
LANES = 128
POWER = 14
SMALLEST = 1e-30
CHUNKS = 4
EARLY = 9 / 16
F32, BF16 = jnp.float32, jnp.bfloat16


VMEM = pl.BlockSpec(memory_space=pltpu.VMEM)
SMEM = pl.BlockSpec(memory_space=pltpu.SMEM)
ANY = pl.BlockSpec(memory_space=pl.ANY)
HBM = pl.BlockSpec(memory_space=pltpu.HBM)


def params(mebibytes):
    return pltpu.CompilerParams(vmem_limit_bytes=mebibytes * 1024 * 1024)


def near(values):
    return pltpu.with_memory_space_constraint(values, pltpu.VMEM)


def far(values):
    return pltpu.with_memory_space_constraint(values, pltpu.HBM)


def exponent_of(top):
    return jnp.floor(jnp.log2(jnp.maximum(top, SMALLEST))) - 8.0


def encode(scaled):
    square = scaled * scaled
    fourth = square * square
    return (fourth * fourth * fourth * (scaled * jnp.abs(scaled))).astype(BF16)


def decode(coded):
    wide = coded.astype(F32)
    size = jnp.abs(wide)
    root = jnp.exp2(jnp.log2(jnp.maximum(size, 1e-37)) * (1.0 / POWER))
    return jnp.where(size == 0.0, 0.0, jnp.where(wide < 0.0, -root, root))


def split(values):
    high = values.astype(BF16)
    return high, (values - high.astype(F32)).astype(BF16)


def dot3(left, right):
    dot = lambda a, b: jnp.dot(a, b, preferred_element_type=F32)
    return dot(left[0], right[0]) + (dot(left[0], right[1]) + dot(left[1], right[0]))


def fold(values):
    rows, columns = values.shape
    return jnp.sum(values.reshape(rows // 8, 8, columns), axis=0)


def parts_of(rows):
    early = int(rows * EARLY) // 32 * 32
    return ((0, early // 2), (early // 2, early)), ((early, (early + rows) // 2), ((early + rows) // 2, rows))


def pack_kernel(group, left_ref, code_ref, left, sems, others=()):
    depth, columns = left.shape
    origin = group[0][0]
    fetches = []
    for start, stop in group:
        here = pl.ds(start - origin, stop - start)
        source = left_ref.at[pl.ds(start, stop - start)]
        fetches.append(pltpu.make_async_copy(source, left.at[here], sems.at[len(fetches)]))
        fetches[-1].start()
    for other in others:
        other.start()
    tails = []
    for start, stop in group:
        here = slice(start - origin, stop - origin)
        fetches.pop(0).wait()
        values = left[here]
        exponent = exponent_of(jnp.max(jnp.abs(values), axis=(0, 1), keepdims=True))
        code = encode(values * jnp.exp2(-exponent))
        for tile in range(columns // LANES):
            first = tile * depth
            code_ref[first + start - origin : first + stop - origin] = code[
                :, tile * LANES : (tile + 1) * LANES
            ]
        tails.append(jnp.broadcast_to(exponent, (TAIL, LANES)))
    lane = lax.broadcasted_iota(jnp.int32, (TAIL, LANES), 1)
    code_ref[columns // LANES * depth :] = jnp.where(lane < LANES // 2, *tails).astype(BF16)


def front_kernel(group, left_ref, partials_ref, code_ref, turned_ref, left, partials, sems, partial_sems):
    parts = partial_sems.shape[0]
    blocks = partials.shape[0]
    per = blocks // parts
    fetches = []
    for part in range(parts):
        here = pl.ds(part * per, per)
        fetches.append(pltpu.make_async_copy(partials_ref.at[here], partials.at[here], partial_sems.at[part]))
    pack_kernel(group, left_ref, code_ref, left, sems, fetches)
    for part in range(parts):
        fetches[part].wait()
        for block in range(part * per, (part + 1) * per):
            turned_ref[blocks - 1 - block] = partials[block]


def front(left, partials):
    columns = left.shape[1]
    group = parts_of(left.shape[0])[0]
    depth = group[1][1] - group[0][0]

    def kernel(*refs):
        front_kernel(group, *refs)

    return pl.pallas_call(
        kernel,
        in_specs=[HBM, HBM],
        out_specs=[VMEM, VMEM],
        out_shape=[
            jax.ShapeDtypeStruct((columns // LANES * depth + TAIL, LANES), BF16),
            pltpu.VMEM(partials.shape, BF16),
        ],
        scratch_shapes=[
            pltpu.VMEM((depth, columns), F32),
            pltpu.VMEM(partials.shape, BF16),
            pltpu.SemaphoreType.DMA((2,)),
            pltpu.SemaphoreType.DMA((2,)),
        ],
        compiler_params=params(16),
    )(far(left), far(partials))


def pack(left, which):
    columns = left.shape[1]
    group = parts_of(left.shape[0])[which]
    depth = group[1][1] - group[0][0]

    def kernel(*refs):
        pack_kernel(group, *refs)

    return pl.pallas_call(
        kernel,
        in_specs=[HBM],
        out_specs=VMEM,
        out_shape=jax.ShapeDtypeStruct((columns // LANES * depth + TAIL, LANES), BF16),
        scratch_shapes=[pltpu.VMEM((depth, columns), F32), pltpu.SemaphoreType.DMA((2,))],
        compiler_params=params(16),
    )(far(left))


def root_of(code_ref, group):
    origin, end = group[0][0], group[1][1]
    depth = end - origin
    tiles = (code_ref.shape[0] - TAIL) // depth
    scales = jnp.exp2(code_ref[tiles * depth :].astype(F32)[0:1])
    rows = []
    for part, (start, stop) in enumerate(group):
        lane = part * (LANES // 2)
        columns = [
            decode(code_ref[tile * depth + start - origin : tile * depth + stop - origin])
            for tile in range(tiles)
        ]
        rows.append(jnp.concatenate(columns, axis=1) * scales[:, lane : lane + 1])
    return jnp.concatenate(rows, axis=0)


def double_kernel(turned_ref, doubled_ref, sems):
    writes = []
    for copy in range(2):
        writes.append(pltpu.make_async_copy(turned_ref, doubled_ref.at[:, copy], sems.at[copy]))
        writes[-1].start()
    for write in writes:
        write.wait()


def double(turned):
    blocks, slab, size = turned.shape
    return pl.pallas_call(
        double_kernel,
        in_specs=[VMEM],
        out_specs=HBM,
        out_shape=pltpu.HBM((blocks, 2, slab, size), BF16),
        scratch_shapes=[pltpu.SemaphoreType.DMA((2,))],
        compiler_params=params(16),
    )(near(turned))


def coded(shampoo, slab, sent, facts, first):
    rows, half = shampoo.shape
    messages = rows // slab
    grouped = shampoo.reshape(messages, slab, half)
    exponent = exponent_of(jnp.max(jnp.abs(grouped), axis=(1, 2), keepdims=True))
    code = encode(grouped * jnp.exp2(-exponent))
    wide = jnp.broadcast_to(exponent, (messages, TAIL, LANES)).astype(BF16)
    for message in range(messages):
        place = first + (messages - 1 - message)
        for tile in range(half // LANES):
            sent[place, tile * slab : (tile + 1) * slab, :] = code[
                message, :, tile * LANES : (tile + 1) * LANES
            ]
        facts[place] = wide[message]
    return fold(shampoo * shampoo)


def main_kernel(
    side_ref, right_ref, pieces_ref, moment_ref, left_ref, code_ref,
    grad_ref, new_ref, sent, turn_hi, turn_lo, facts_ref, sums_ref,
    pieces, moment, left, grad, new, right_hi, right_lo, fetch_sems, write_sems,
):
    side = side_ref[0]
    blocks, _, slab, size = pieces.shape
    half = size // 2
    chunks = CHUNKS
    rows = size // chunks
    messages = rows // slab
    early = parts_of(half)[0]

    def fetch(source, target, slot):
        copy = pltpu.make_async_copy(source, target, fetch_sems.at[slot])
        copy.start()
        return copy

    def fetch_pieces(chunk):
        here = pl.ds(blocks - (chunk + 1) * messages, messages)
        return fetch(pieces_ref.at[here], pieces.at[here], chunk)

    def fetch_moment(chunk):
        here = pl.ds(chunk * rows, rows)
        return fetch(moment_ref.at[here], moment.at[here], chunks + chunk)

    piece_arrivals = [fetch_pieces(chunk) for chunk in range(chunks)]
    moment_arrivals = [fetch_moment(chunk) for chunk in range(chunks)]
    writes = []

    def write(source, target):
        writes.append(pltpu.make_async_copy(source, target, write_sems.at[len(writes)]))
        writes[-1].start()

    right_hi[...], right_lo[...] = split(right_ref[...])
    adam = jnp.zeros((8, half), F32)
    for chunk in range(chunks):
        here = slice(chunk * rows, (chunk + 1) * rows)
        piece_arrivals[chunk].wait()
        if chunk == 0:
            left_arrival = fetch(left_ref, left, 2 * chunks)
        for message in range(messages):
            source = chunk * messages + message
            piece = blocks - 1 - source
            grad[source * slab : (source + 1) * slab] = pieces[piece, 0].astype(F32) + pieces[
                piece, 1
            ].astype(F32)
        write(grad.at[pl.ds(chunk * rows, rows)], grad_ref.at[pl.ds(chunk * rows, rows)])
        turned = dot3(split(grad[here]), (right_hi[...], right_lo[...]))
        turn_hi[here], turn_lo[here] = split(turned)
        mine = grad[here, pl.ds(pl.multiple_of(side * half, half), half)]
        moment_arrivals[chunk].wait()
        moment_new = MOMENT_DECAY * moment[here] + (1.0 - MOMENT_DECAY) * mine * mine
        new[here] = moment_new
        direction = mine / (moment_new * lax.rsqrt(moment_new) + ADAM_EPS)
        adam += fold(direction * direction)
    write(new, new_ref)

    def finish(left, row_block):
        shampoo = dot3(split(left), (turn_hi[...], turn_lo[...]))
        count = left.shape[0] // slab
        first = blocks - count - row_block
        return coded(shampoo, slab, sent, facts_ref, first)

    squares = jnp.zeros((8, half), F32)
    left_arrival.wait()
    for start in range(0, half, rows):
        squares += finish(left[start : start + rows], side * (blocks // 2) + start // slab)
    squares += finish(root_of(code_ref, early), (1 - side) * (blocks // 2))
    sums_ref[:8] = adam
    sums_ref[8:] = squares
    for copy in writes:
        copy.wait()


def main(side, pieces, moment, right, left, code):
    size, half = right.shape
    blocks, _, slab, _ = pieces.shape
    data = half // LANES * slab
    return pl.pallas_call(
        main_kernel,
        in_specs=[SMEM, VMEM, HBM, HBM, HBM, VMEM],
        out_specs=[HBM, ANY, VMEM, VMEM, VMEM, VMEM, VMEM],
        out_shape=[
            pltpu.HBM((size, size), F32),
            jax.ShapeDtypeStruct((size, half), F32),
            pltpu.VMEM((blocks, data, LANES), BF16),
            pltpu.VMEM((size, half), BF16),
            pltpu.VMEM((size, half), BF16),
            pltpu.VMEM((blocks, TAIL, LANES), BF16),
            pltpu.VMEM((16, half), F32),
        ],
        scratch_shapes=[
            pltpu.VMEM(pieces.shape, BF16),
            pltpu.VMEM(moment.shape, F32),
            pltpu.VMEM(left.shape, F32),
            pltpu.VMEM((size, size), F32),
            pltpu.VMEM(moment.shape, F32),
            pltpu.VMEM((size, half), BF16),
            pltpu.VMEM((size, half), BF16),
            pltpu.SemaphoreType.DMA((2 * CHUNKS + 1,)),
            pltpu.SemaphoreType.DMA((CHUNKS + 1,)),
        ],
        compiler_params=params(36),
        cost_estimate=pl.CostEstimate(
            flops=12 * size * size * half, bytes_accessed=16 * size * size, transcendentals=4 * size * half
        ),
    )(side, near(right), far(pieces), far(moment), far(left), near(code))


def last_kernel(side_ref, turn_hi, turn_lo, code_ref, facts_ref, sums_ref, done_ref, sent_ref, sent, facts, sems):
    side = side_ref[0]
    blocks = facts.shape[0]
    slab = 16
    data = sent.shape[1]
    half = turn_hi.shape[1]
    late = parts_of(half)[1]
    count = sent.shape[0]
    row_block = (1 - side) * (blocks // 2) + late[0][0] // slab
    first = blocks - count - row_block

    writes = []

    def write(source, target):
        writes.append(pltpu.make_async_copy(source, target, sems.at[len(writes)]))
        writes[-1].start()

    rest = blocks // 2 - count
    for start, extent in (((1 - side) * (blocks // 2), blocks // 2), (first + count, rest)):
        here = pl.ds(start, extent)
        write(done_ref.at[here], sent_ref.at[here, pl.ds(0, data)])
    facts[...] = facts_ref[...]
    shampoo = dot3(split(root_of(code_ref, late)), (turn_hi[...], turn_lo[...]))
    squares = coded(shampoo, slab, sent, facts.at[pl.ds(first, count)], 0)
    write(sent, sent_ref.at[pl.ds(first, count), pl.ds(0, data)])

    values = facts[...]
    lane = lax.broadcasted_iota(jnp.int32, values.shape, 2)
    place = 1
    for total in (sums_ref[:8], sums_ref[8:] + squares):
        rest = jnp.sum(total, axis=(0, 1), keepdims=True)
        for _ in range(3):
            piece = rest.astype(BF16)
            rest = rest - piece.astype(F32)
            values = jnp.where(lane == place, piece.reshape(1, 1, 1), values)
            place += 1
    facts[...] = values
    write(facts, sent_ref.at[:, pl.ds(data, TAIL)])
    for copy in writes:
        copy.wait()


def last(side, turn_hi, turn_lo, code, facts, sums, done):
    size, half = turn_hi.shape
    blocks, data, lanes = done.shape
    (start, _), (_, stop) = parts_of(half)[1]
    return pl.pallas_call(
        last_kernel,
        in_specs=[SMEM] + [VMEM] * 6,
        out_specs=HBM,
        out_shape=pltpu.HBM((blocks, data + TAIL, lanes), BF16),
        scratch_shapes=[
            pltpu.VMEM(((stop - start) // 16, data, LANES), BF16),
            pltpu.VMEM(facts.shape, BF16),
            pltpu.SemaphoreType.DMA((4,)),
        ],
        compiler_params=params(16),
        cost_estimate=pl.CostEstimate(
            flops=6 * size * half * (stop - start), bytes_accessed=8 * size * half, transcendentals=0
        ),
    )(side, near(turn_hi), near(turn_lo), near(code), near(facts), near(sums), near(done))


def facts_kernel(got_ref, o_ref):
    depth = got_ref.shape[1]
    o_ref[...] = got_ref[:, depth - TAIL :, :].astype(F32)[:, 0, :]


def facts_of(got):
    blocks, _, lanes = got.shape
    return pl.pallas_call(
        facts_kernel,
        in_specs=[VMEM],
        out_specs=VMEM,
        out_shape=pltpu.VMEM((blocks, lanes), F32),
        compiler_params=params(16),
    )(near(got))


def unpack_kernel(got_ref, o_ref):
    blocks, slab, columns = o_ref.shape
    for tile in range(columns // LANES):
        values = decode(got_ref[:, tile * slab : (tile + 1) * slab, :])
        for block in range(blocks):
            o_ref[block, :, tile * LANES : (tile + 1) * LANES] = values[blocks - 1 - block]


def unpack(got, slab):
    blocks, depth, lanes = got.shape
    return pl.pallas_call(
        unpack_kernel,
        in_specs=[VMEM],
        out_specs=VMEM,
        out_shape=pltpu.VMEM((blocks, slab, (depth - TAIL) // slab * lanes), F32),
        compiler_params=params(16),
        cost_estimate=pl.CostEstimate(
            flops=20 * blocks * depth * lanes, bytes_accessed=8 * blocks * depth * lanes, transcendentals=0
        ),
    )(near(got))


def scale_kernel(entries, values_ref, mine_ref, other_ref, o_ref, scaled, sems):
    blocks = values_ref.shape[0]
    mine = mine_ref[...]
    both = mine + other_ref[...]
    total = lambda k: (both[:, k : k + 1] + both[:, k + 1 : k + 2]) + both[:, k + 2 : k + 3]
    ratio = jnp.sqrt(total(1) / entries + NORM_EPS) / jnp.sqrt(total(4) / entries + NORM_EPS)
    factor = ratio * jnp.exp2(mine[:, 0:1])
    parts = sems.shape[0]
    per = blocks // parts
    writes = []
    for part in range(parts):
        for block in range(part * per, (part + 1) * per):
            source = blocks - 1 - block
            scaled[block] = values_ref[block] * factor[source : source + 1]
        here = pl.ds(part * per, per)
        writes.append(pltpu.make_async_copy(scaled.at[here], o_ref.at[here], sems.at[part]))
        writes[-1].start()
    for write in writes:
        write.wait()


def rescale(values, mine, other, entries):
    def kernel(*refs):
        scale_kernel(entries, *refs)

    return pl.pallas_call(
        kernel,
        in_specs=[VMEM] * 3,
        out_specs=ANY,
        out_shape=jax.ShapeDtypeStruct(values.shape, F32),
        scratch_shapes=[pltpu.VMEM(values.shape, F32), pltpu.SemaphoreType.DMA((8,))],
        compiler_params=params(16),
    )(near(values), mine, other)


def highest(form, left, right):
    return jnp.einsum(form, left, right, precision=lax.Precision.HIGH, preferred_element_type=F32)


def local(grad_partials, second_moment, left_root, right_root, left_stat, right_stat):
    partials = grad_partials[0]
    blocks, slab, size = partials.shape
    half = size // 2
    side = lax.axis_index("dp")

    left = left_root[0]
    early, turned = front(left, partials)
    early = lax.ppermute(early, "dp", SWAP)

    def deliver(values, left):
        pieces = lax.all_to_all(
            values.reshape(2 * blocks, slab, size),
            ("mp", "dp"),
            split_axis=0,
            concat_axis=0,
            tiled=True,
            axis_index_groups=[list(range(2 * blocks))[::-1]],
        )
        return pieces, pack(left, 1)

    def nothing(values, left):
        shapes = jax.eval_shape(lambda: (jnp.zeros((2 * blocks, slab, size), values.dtype), pack(left, 1)))
        return tuple(jnp.zeros(each.shape, each.dtype) for each in shapes)

    pieces, late = lax.cond((side + 2) // 2 == 1, deliver, nothing, double(turned), left)
    pieces = pieces.reshape(blocks, 2, slab, size)
    late = lax.ppermute(late, "dp", SWAP)
    where = side.astype(jnp.int32).reshape(1)
    grad, moment_new, sent, turn_hi, turn_lo, facts, sums = main(
        where, pieces, second_moment[0], right_root[0], left, early
    )
    sent = last(where, turn_hi, turn_lo, late, facts, sums, sent)
    got = lax.all_to_all(
        sent, "mp", split_axis=0, concat_axis=0, tiled=True, axis_index_groups=[list(range(blocks))[::-1]]
    )
    scale = (1.0 - STAT_DECAY) / size
    rows = lax.dynamic_slice_in_dim(grad, side * half, half, 0)
    columns = lax.dynamic_slice_in_dim(grad, side * half, half, 1)
    left_new = STAT_DECAY * left_stat[0] + scale * highest("ic,jc->ij", rows, grad)
    right_new = STAT_DECAY * right_stat[0] + scale * highest("ri,rj->ij", grad, columns)
    got, left_new, right_new = lax.optimization_barrier((got, left_new, right_new))
    mine = facts_of(got)
    other = lax.ppermute(mine, "dp", SWAP)
    update = rescale(unpack(got, slab), mine, other, float(size * size))
    return (update, moment_new[None], left_new[None], right_new[None])


def solution(mesh):
    return jax.shard_map(
        local,
        mesh=mesh,
        in_specs=(
            P("dp", None, "mp", None),
            P("mp", None, "dp"),
            P("mp", "dp", None),
            P("mp", None, "dp"),
            P("mp", "dp", None),
            P("mp", None, "dp"),
        ),
        out_specs=(
            P(None, "mp", "dp"),
            P("mp", None, "dp"),
            P("mp", "dp", None),
            P("mp", None, "dp"),
        ),
        check_vma=False,
    )
```
